256 devices in a mesh: dp: 32 (over z_hi, x, y), tensor: 8 (over z_lo, core).
Axes of the slice: x: 4, y: 4, z: 8 (z_hi: 2, z_lo: 4; z = z_hi * 4 + z_lo), core: 2. Of those that a mesh axis runs over, the one named last changes fastest.
Arguments:
- hidden_rows: bfloat16 [512, 2, 8192], P('dp', None, 'tensor'), may hold values from -6 to 6
- key_value_weight: bfloat16 [8192, 2048], P(None, 'tensor'), may hold values from -0.0625 to 0.0625
- adapter_down_weight: bfloat16 [128, 8192, 128], P('dp', 'tensor'), may hold values from -0.0625 to 0.0625
- adapter_up_weight: bfloat16 [128, 64, 2048], P('dp', None, 'tensor'), may hold values from -0.75 to 0.75
- adapter_ids: int32 [512], replicated, may hold values from 0 to 127
- kv_lengths: int32 [512], P('dp'), may hold values from 2 to 512, as said below
- queries: bfloat16 [512, 2, 8192], P('dp', None, 'tensor'), may hold values from -120 to 120
- k_cache: bfloat16 [512, 512, 1024], P('dp', None, 'tensor'), may hold values from -6 to 6
- value_cache: bfloat16 [512, 512, 1024], P('dp', None, 'tensor'), may hold values from -6 to 6
Outputs:
- new_kv: bfloat16 [512, 2, 2048], P('dp', None, 'tensor')
- attended: bfloat16 [512, 2, 8192], P('dp', None, 'tensor')
The draws below stay inside these ranges and needn't reach their ends.
Inputs may be any that keep to these rules, and one draw needn't show every extreme that they name: `kv_lengths`: at least one row has exactly 512 positions in use.
All inputs are finite; a program needn't handle non-finite values.
Results may differ from the reference program's by a relative error of at most 0.0057.
Values may be sent and summed in bfloat16 or wider, within the bound.
No kernel may reach another device: no remote copies, remote signals or barrier semaphores. Data moves between devices by JAX's collectives and lax.ppermute only.
A program may use at most 128 MiB of HBM per device.

```python
import math
import jax
import jax.numpy as jnp
import numpy as np
from jax import lax

MODEL_WIDTH = 8192
QUERY_HEADS = 64
KEY_VALUE_HEADS = 8
HEAD_SIZE = 128
ADAPTER_RANK = 64
DECODE_STEPS = 2
CACHE_POSITIONS = 512
DECODE_ROWS = 512
ADAPTER_POOL = 128


def first_keys(key):
    return jnp.clip(jax.random.normal(jax.random.fold_in(key, 77), (DECODE_ROWS, KEY_VALUE_HEADS * HEAD_SIZE), jnp.float32), -6.0, 6.0)


def draw_k_cache(key, part):
    shared_weight = first_keys(key)
    key = jax.random.fold_in(key, 3)
    key_cache_rows = jnp.clip(jax.random.normal(key, (DECODE_ROWS, CACHE_POSITIONS, KEY_VALUE_HEADS * HEAD_SIZE), jnp.float32), -6.0, 6.0)
    key_cache_rows = key_cache_rows.at[:, 0, :].set(shared_weight)
    return key_cache_rows.astype(jnp.bfloat16)


def draw_queries(key, part):
    key = jax.random.fold_in(key, 4)
    query_group_size = QUERY_HEADS // KEY_VALUE_HEADS
    drawn_projection = jnp.clip(jax.random.normal(key, (DECODE_ROWS, DECODE_STEPS, KEY_VALUE_HEADS, query_group_size, HEAD_SIZE), jnp.float32), -6.0, 6.0)
    return drawn_projection.reshape(DECODE_ROWS, DECODE_STEPS, QUERY_HEADS * HEAD_SIZE).astype(jnp.bfloat16)


def draw_kv_lengths(key, part):
    key = jax.random.fold_in(key, 5)
    key_left, key_right, key_full = jax.random.split(key, 3)
    left_part = jax.random.randint(key_left, (DECODE_ROWS,), 0, CACHE_POSITIONS - 1)
    right_part = jax.random.randint(key_right, (DECODE_ROWS,), 0, CACHE_POSITIONS - 1)
    lengths = 2 + left_part * right_part // (CACHE_POSITIONS - 2)
    full_row = jax.random.randint(key_full, (), 0, DECODE_ROWS)
    lengths = jnp.where(jnp.arange(DECODE_ROWS) == full_row, CACHE_POSITIONS, lengths)
    return lengths.astype(jnp.int32)


def place_ends(drawn, own_key, smallest, largest):
    shape = drawn.shape
    index_at = [jax.random.randint(jax.random.fold_in(own_key, axis), (), 0, shape[axis]) for axis in range(len(shape))]
    drawn = drawn.at[tuple(index_at)].set(smallest)
    longest = shape.index(max(shape))
    index_at[longest] = (index_at[longest] + 1) % shape[longest]
    return drawn.at[tuple(index_at)].set(largest)


def shard_levels(key, dims, cuts, smallest, high):
    loudness, own = 1.0, jax.random.fold_in(key, 6)
    for position, shards_of in cuts:
        steps = jnp.exp(jax.random.uniform(jax.random.fold_in(own, position), (shards_of,), jnp.float32, smallest / len(cuts), high / len(cuts)))
        loudness = loudness * jnp.repeat(steps, dims[position] // shards_of).reshape([-1 if axis == position else 1 for axis in range(len(dims))])
    return loudness


def rank_table(number_of, lean):
    portions = [(1 << 20) // math.isqrt(standing ** lean) + 1 for standing in range(1, number_of + 1)]
    deviation = 1 + sum(portions) // (1 << 30)
    return np.cumsum(np.array([max(1, weight // deviation) for weight in portions]))


def ranked_ids(key, extent, number_of, lean):
    table = rank_table(number_of, lean)
    pick = jax.random.randint(jax.random.fold_in(key, 1), extent, 0, int(table[number_of - 1]))
    grade = jnp.searchsorted(jnp.asarray(table, jnp.int32), pick, side="right")
    return jax.random.permutation(jax.random.fold_in(key, 2), number_of)[grade].astype(jnp.int32)


def centred(stream_key, dims, scale, most, pieces=(), held_as=jnp.bfloat16):
    values = scale * jax.random.normal(stream_key, dims, jnp.float32)
    if pieces:
        values = values * shard_levels(stream_key, dims, pieces, -0.22, 0.18)
    return jnp.clip(values, -most, most).astype(held_as)


def setup_inputs(seed: int = 0) -> dict:
    arg_keys = jax.random.split(jax.random.key(seed), 10)
    hidden_rows = centred(arg_keys[0], (DECODE_ROWS, DECODE_STEPS, MODEL_WIDTH), 1.0, 6.0, ((0, 32), (2, 8)))
    key_value_weight = centred(arg_keys[1], (MODEL_WIDTH, 2 * KEY_VALUE_HEADS * HEAD_SIZE), MODEL_WIDTH ** -0.5, 0.0625, ((1, 8),))
    adapter_down_weight = centred(arg_keys[2], (ADAPTER_POOL, MODEL_WIDTH, 2 * ADAPTER_RANK), MODEL_WIDTH ** -0.5, 0.0625, ((0, 32), (1, 8)))
    adapter_up_weight = centred(arg_keys[3], (ADAPTER_POOL, ADAPTER_RANK, 2 * KEY_VALUE_HEADS * HEAD_SIZE), ADAPTER_RANK ** -0.5, 0.75, ((0, 32), (2, 8)))
    adapter_ids = place_ends(ranked_ids(arg_keys[4], (DECODE_ROWS,), ADAPTER_POOL, 2), jax.random.fold_in(arg_keys[4], 3), 0, ADAPTER_POOL - 1).astype(jnp.int32)
    kv_lengths = draw_kv_lengths(jax.random.fold_in(arg_keys[9], 71), 0)
    queries = draw_queries(jax.random.fold_in(arg_keys[9], 71), 0)
    k_cache = draw_k_cache(jax.random.fold_in(arg_keys[9], 71), 0)
    value_cache = centred(arg_keys[8], (DECODE_ROWS, CACHE_POSITIONS, KEY_VALUE_HEADS * HEAD_SIZE), 1.0, 6.0, ((0, 32), (2, 8)))
    return {"hidden_rows": hidden_rows, "key_value_weight": key_value_weight, "adapter_down_weight": adapter_down_weight, "adapter_up_weight": adapter_up_weight, "adapter_ids": adapter_ids, "kv_lengths": kv_lengths, "queries": queries, "k_cache": k_cache, "value_cache": value_cache}


def rotate(keys_in, positions):
    half_width = keys_in.shape[-1] // 2
    frequency = jnp.exp(jnp.arange(half_width, dtype=jnp.float32) * (-2.0 * math.log(500000.0) / keys_in.shape[-1]))
    angles = positions.astype(jnp.float32)[..., None, None] * frequency
    cosine = jnp.cos(angles)
    sine_part = jnp.sin(angles)
    lower_half = keys_in[..., :half_width]
    upper_half = keys_in[..., half_width:]
    return jnp.concatenate([lower_half * cosine - upper_half * sine_part, upper_half * cosine + lower_half * sine_part], -1)

def reference(hidden_rows, key_value_weight, adapter_down_weight, adapter_up_weight, adapter_ids, kv_lengths, queries, k_cache, value_cache):
    query_group_size = QUERY_HEADS // KEY_VALUE_HEADS
    score_scale = 1.0 / math.sqrt(HEAD_SIZE)

    def one_row(row_item):
        feature_vector, identity_matrix, length, query_vector, previous_keys, previous_values = row_item
        base_projection = jnp.dot(feature_vector, key_value_weight, preferred_element_type=jnp.float32).reshape(DECODE_STEPS, KEY_VALUE_HEADS, 2, HEAD_SIZE)
        adapter_down_rows = jnp.dot(feature_vector, adapter_down_weight[identity_matrix], preferred_element_type=jnp.float32).astype(jnp.bfloat16)
        adapter_down_rows = lax.optimization_barrier(adapter_down_rows).astype(jnp.float32)
        up_weight_table = adapter_up_weight[identity_matrix].astype(jnp.float32).reshape(ADAPTER_RANK, KEY_VALUE_HEADS, 2, HEAD_SIZE)
        key_update = jnp.einsum('cx,xne->cne', adapter_down_rows[:, :ADAPTER_RANK], up_weight_table[:, :, 0])
        value_update = jnp.einsum('cx,xne->cne', adapter_down_rows[:, ADAPTER_RANK:], up_weight_table[:, :, 1])
        positions = length + jnp.arange(DECODE_STEPS, dtype=jnp.int32)
        keys_new = rotate(base_projection[:, :, 0] + key_update, positions)
        values_new = base_projection[:, :, 1] + value_update
        fresh_key_value = jnp.stack([keys_new, values_new], 2).astype(jnp.bfloat16)
        fresh_keys = fresh_key_value[:, :, 0].astype(jnp.float32)
        fresh_values = fresh_key_value[:, :, 1].astype(jnp.float32)
        query_head_count = query_vector.astype(jnp.float32).reshape(DECODE_STEPS, KEY_VALUE_HEADS, query_group_size, HEAD_SIZE)
        stored_keys = previous_keys.astype(jnp.float32).reshape(CACHE_POSITIONS, KEY_VALUE_HEADS, HEAD_SIZE)
        stored_values = previous_values.astype(jnp.float32).reshape(CACHE_POSITIONS, KEY_VALUE_HEADS, HEAD_SIZE)
        old_scores = jnp.einsum('shgd,jhd->shgj', query_head_count, stored_keys) * score_scale
        valid_mask = jnp.arange(CACHE_POSITIONS, dtype=jnp.int32) < length
        old_scores = jnp.where(valid_mask, old_scores, -jnp.inf)
        new_scores = jnp.einsum('shgd,thd->shgt', query_head_count, fresh_keys) * score_scale
        causal_mask = jnp.arange(DECODE_STEPS)[None, :] <= jnp.arange(DECODE_STEPS)[:, None]
        new_scores = jnp.where(causal_mask[:, None, None, :], new_scores, -jnp.inf)
        scores = jnp.concatenate([old_scores, new_scores], -1)
        row_max = lax.optimization_barrier(jnp.max(scores, -1, keepdims=True))
        exponent = jnp.exp(scores - row_max)
        weights = (exponent / lax.optimization_barrier(jnp.sum(exponent, -1, keepdims=True))).astype(jnp.bfloat16)
        weights = lax.optimization_barrier(weights).astype(jnp.float32)
        attention_output = jnp.einsum('shgj,jhd->shgd', weights[..., :CACHE_POSITIONS], stored_values)
        attention_output = attention_output + jnp.einsum('shgt,thd->shgd', weights[..., CACHE_POSITIONS:], fresh_values)
        return (fresh_key_value.reshape(DECODE_STEPS, 2 * KEY_VALUE_HEADS * HEAD_SIZE), attention_output.astype(jnp.bfloat16).reshape(DECODE_STEPS, QUERY_HEADS * HEAD_SIZE))
    new_kv, attended = lax.map(one_row, (hidden_rows, adapter_ids, kv_lengths, queries, k_cache, value_cache))
    return (new_kv, attended)
```

```python
import math

import jax
import jax.numpy as jnp
from jax import lax
from jax.sharding import PartitionSpec as P

HEAD_SIZE = 128
F32 = jnp.float32
BF16 = jnp.bfloat16
BOTH = ("dp", "tensor")


def pairs_of(move):
    pairs = []
    for d in range(32):
        for j in range(8):
            z, x, y, t, c = d // 16, d // 4 % 4, d % 4, j // 2, j % 2
            z, x, y, t, c = move(z, x, y, t, c)
            pairs.append((d * 8 + j, (z * 16 + x * 4 + y) * 8 + t * 2 + c))
    return pairs


def swap_core(value):
    return lax.ppermute(value, BOTH, pairs_of(lambda z, x, y, t, c: (z, x, y, t, c ^ 1)))


def cross_z(value):
    return lax.ppermute(value, BOTH, pairs_of(lambda z, x, y, t, c: (z ^ c, x, y, t, c)))


def first_axis(value, k):
    return lax.ppermute(
        value,
        BOTH,
        pairs_of(lambda z, x, y, t, c: (z, x ^ (0 if c else k), y ^ (k if c else 0), t, c)),
    )


def second_axis(value, k):
    return lax.ppermute(
        value,
        BOTH,
        pairs_of(lambda z, x, y, t, c: (z, x ^ (k if c else 0), y ^ (0 if c else k), t, c)),
    )


def along_z(value, k):
    return lax.ppermute(value, BOTH, pairs_of(lambda z, x, y, t, c: (z, x, y, t ^ k, c)))


def cached_attention(queries, k_cache, value_cache, kv_lengths):
    rows, context = k_cache.shape[0], k_cache.shape[1]
    scores = jnp.einsum("rqd,rjd->rqj", queries, k_cache, preferred_element_type=F32)
    scores = scores * (1.0 / math.sqrt(HEAD_SIZE))
    valid = jnp.arange(context, dtype=jnp.int32)[None, :] < kv_lengths[:, None]
    scores = jnp.where(valid[:, None, :], scores, -jnp.inf)
    top = jnp.max(scores, -1, keepdims=True)
    weight = jnp.exp(scores - top)
    total = jnp.sum(weight, -1, keepdims=True)
    gathered = jnp.einsum(
        "rqj,rjd->rqd", weight.astype(BF16), value_cache, preferred_element_type=F32
    )
    return top, total, gathered


def per_device(
    hidden_rows,
    key_value_weight,
    adapter_down_weight,
    adapter_up_weight,
    adapter_ids,
    kv_lengths,
    queries,
    k_cache,
    value_cache,
):
    rows, steps, width = hidden_rows.shape
    owned = adapter_down_weight.shape[0]
    rank = adapter_down_weight.shape[2] // 2
    group = rows * steps
    me = lax.axis_index("dp")
    j = lax.axis_index("tensor")
    t, c = j // 2, j % 2

    own = hidden_rows.reshape(group, width)
    pair = jnp.concatenate([own, swap_core(own)], 1)
    down_weight = jnp.concatenate([adapter_down_weight, swap_core(adapter_down_weight)], 1)
    up_other = swap_core(adapter_up_weight)

    start = cross_z(pair)
    line = jnp.concatenate([start] + [first_axis(start, k) for k in (1, 2, 3)], 0)
    blocks = {0: line}
    for k in (1, 3, 2):
        blocks[k] = second_axis(line, k)

    k2 = jnp.arange(4, dtype=jnp.int32)[:, None]
    k1 = jnp.arange(4, dtype=jnp.int32)[None, :]
    groups = me ^ (16 * c) ^ jnp.where(c == 0, 4 * k1 + k2, 4 * k2 + k1)
    ids = adapter_ids.reshape(32, rows)[groups]
    hot = ids[..., None] == me * owned + jnp.arange(owned, dtype=jnp.int32)
    hot = jnp.repeat(hot, steps, axis=2).reshape(4, 4 * group, owned)

    partial = []
    for k in range(4):
        products = jnp.einsum("rd,adk->rak", blocks[k], down_weight, preferred_element_type=F32)
        partial.append(jnp.sum(jnp.where(hot[k][:, :, None], products, 0.0), axis=1))
    partial = jnp.stack(partial)

    mine = lax.dynamic_index_in_dim(partial, t, 0, keepdims=False)
    rounded = partial.astype(BF16)
    for m in (1, 2, 3):
        sent = lax.dynamic_index_in_dim(rounded, t ^ m, 0, keepdims=False)
        mine = mine + along_z(sent, m).astype(F32)
    mine = mine.astype(BF16)
    low = jnp.stack([mine] + [along_z(mine, m) for m in (1, 2, 3)])

    hot_slots = jnp.stack([lax.dynamic_index_in_dim(hot, t ^ m, 0, keepdims=False) for m in range(4)])
    spread = jnp.where(hot_slots[..., None], low[:, :, None, :], 0.0).astype(BF16)
    spread_key = spread[..., :rank].reshape(-1, owned * rank)
    spread_value = spread[..., rank:].reshape(-1, owned * rank)

    def up_columns(first):
        columns = [
            u[:, :, first : first + HEAD_SIZE].reshape(owned * rank, HEAD_SIZE)
            for u in (adapter_up_weight, up_other)
        ]
        return jnp.concatenate(columns, 1)

    delta_key = jnp.dot(spread_key, up_columns(0), preferred_element_type=F32).astype(BF16)
    delta_value = jnp.dot(spread_value, up_columns(HEAD_SIZE), preferred_element_type=F32).astype(
        BF16
    )
    delta = jnp.concatenate(
        [
            delta_key[:, :HEAD_SIZE],
            delta_value[:, :HEAD_SIZE],
            delta_key[:, HEAD_SIZE:],
            delta_value[:, HEAD_SIZE:],
        ],
        1,
    ).reshape(4, 4 * group, 4 * HEAD_SIZE)

    back = lax.dynamic_index_in_dim(delta, t, 0, keepdims=False)
    for k in (1, 3, 2):
        back = back + second_axis(lax.dynamic_index_in_dim(delta, t ^ k, 0, keepdims=False), k)
    back = back.reshape(4, group, 4 * HEAD_SIZE)
    home = back[0]
    for k in (1, 3, 2):
        home = home + first_axis(back[k], k)
    home = cross_z(home)
    update = home[:, : 2 * HEAD_SIZE] + swap_core(home[:, 2 * HEAD_SIZE :])

    chips = [pair] + [along_z(pair, m) for m in (1, 2, 3)]
    full = jnp.zeros((4, 2, group, width), BF16)
    for m in range(4):
        both = jnp.stack([chips[m][:, :width], chips[m][:, width:]])
        both = jnp.where(c == 0, both, both[::-1])
        full = lax.dynamic_update_slice(full, both[None], (t ^ m, 0, 0, 0))
    full = full.transpose(2, 0, 1, 3).reshape(group, 8 * width)
    base = jnp.dot(full, key_value_weight, preferred_element_type=F32)

    projected = (base + update.astype(F32)).reshape(rows, steps, 2, HEAD_SIZE)
    half = HEAD_SIZE // 2
    frequency = jnp.exp(
        jnp.arange(half, dtype=F32) * (-2.0 * math.log(500000.0) / HEAD_SIZE)
    )
    positions = kv_lengths[:, None] + jnp.arange(steps, dtype=jnp.int32)[None, :]
    angles = positions.astype(F32)[..., None] * frequency
    cosine, sine = jnp.cos(angles), jnp.sin(angles)
    low_half, high_half = projected[:, :, 0, :half], projected[:, :, 0, half:]
    key = jnp.concatenate(
        [low_half * cosine - high_half * sine, high_half * cosine + low_half * sine], -1
    )
    fresh = jnp.stack([key, projected[:, :, 1]], 2).astype(BF16)
    new_kv = fresh.reshape(rows, steps, 2 * HEAD_SIZE)
    fresh_key = fresh[:, :, 0].astype(F32)
    fresh_value = fresh[:, :, 1].astype(F32)

    heads = queries.shape[2] // HEAD_SIZE
    q = queries.reshape(rows, steps * heads, HEAD_SIZE)
    top, total, gathered = cached_attention(q, k_cache, value_cache, kv_lengths)
    new_scores = jnp.einsum(
        "rqd,rtd->rqt", q, fresh[:, :, 0], preferred_element_type=F32
    ) * (1.0 / math.sqrt(HEAD_SIZE))
    step_of = jnp.arange(steps * heads, dtype=jnp.int32) // heads
    seen = jnp.arange(steps, dtype=jnp.int32)[None, :] <= step_of[:, None]
    new_scores = jnp.where(seen[None], new_scores, -jnp.inf)
    highest = jnp.maximum(top, jnp.max(new_scores, -1, keepdims=True))
    scale = jnp.exp(top - highest)
    new_weight = jnp.exp(new_scores - highest)
    total = total * scale + jnp.sum(new_weight, -1, keepdims=True)
    result = gathered * scale
    for s in range(steps):
        result = result + new_weight[:, :, s : s + 1] * fresh_value[:, s][:, None, :]
    attended = (result / total).astype(BF16).reshape(rows, steps, heads * HEAD_SIZE)
    return (new_kv, attended)


def solution(mesh):
    return jax.shard_map(
        per_device,
        mesh=mesh,
        in_specs=(
            P("dp", None, "tensor"),
            P(None, "tensor"),
            P("dp", "tensor", None),
            P("dp", None, "tensor"),
            P(),
            P("dp"),
            P("dp", None, "tensor"),
            P("dp", None, "tensor"),
            P("dp", None, "tensor"),
        ),
        out_specs=(P("dp", None, "tensor"), P("dp", None, "tensor")),
        check_vma=False,
    )
```

```python
import math

import jax
import jax.numpy as jnp
from jax import lax
from jax.experimental import pallas as pl
from jax.experimental.pallas import tpu as pltpu
from jax.sharding import PartitionSpec as P

HEAD_SIZE = 128
F32 = jnp.float32
BF16 = jnp.bfloat16
BOTH = ("dp", "tensor")


def pairs_of(move):
    pairs = []
    for d in range(32):
        for j in range(8):
            z, x, y, t, c = d // 16, d // 4 % 4, d % 4, j // 2, j % 2
            z, x, y, t, c = move(z, x, y, t, c)
            pairs.append((d * 8 + j, (z * 16 + x * 4 + y) * 8 + t * 2 + c))
    return pairs


def swap_core(value):
    return lax.ppermute(value, BOTH, pairs_of(lambda z, x, y, t, c: (z, x, y, t, c ^ 1)))


def cross_z(value):
    return lax.ppermute(value, BOTH, pairs_of(lambda z, x, y, t, c: (z ^ c, x, y, t, c)))


def first_axis(value, k):
    return lax.ppermute(
        value,
        BOTH,
        pairs_of(lambda z, x, y, t, c: (z, x ^ (0 if c else k), y ^ (k if c else 0), t, c)),
    )


def second_axis(value, k):
    return lax.ppermute(
        value,
        BOTH,
        pairs_of(lambda z, x, y, t, c: (z, x ^ (k if c else 0), y ^ (0 if c else k), t, c)),
    )


def along_z(value, k):
    return lax.ppermute(value, BOTH, pairs_of(lambda z, x, y, t, c: (z, x, y, t ^ k, c)))


def swap_z(value):
    return lax.ppermute(value, BOTH, pairs_of(lambda z, x, y, t, c: (z ^ 1, x, y, t, c)))


def hbm():
    return pl.BlockSpec(memory_space=pl.ANY)


def vmem():
    return pl.BlockSpec(memory_space=pltpu.VMEM)


def smem():
    return pl.BlockSpec(memory_space=pltpu.SMEM)


def mask_kernel(
    groups_ref, first_ref, ids_ref, up_own_ref, up_other_ref, own_ref, after_ref,
    code_ref, up_ref, same_ref,
):
    first = first_ref[0]
    same_ref[...] = own_ref[...]
    for k2 in range(4):
        for k1 in range(4):
            code_ref[k2, 32 * k1 : 32 * k1 + 32, :] = ids_ref[groups_ref[4 * k2 + k1]] - first
    up_ref[...] = jnp.zeros_like(up_ref)
    for a in range(up_own_ref.shape[0]):
        for n, ref in enumerate((up_own_ref, up_other_ref)):
            at = 2 * HEAD_SIZE * n
            up_ref[128 * a : 128 * a + 64, at : at + 128] = ref[a, :, :128]
            up_ref[128 * a + 64 : 128 * a + 128, at + 128 : at + 256] = ref[a, :, 128:]


def make_masks(groups, first, ids_wide, up_own, up_other, own, after):
    owned = up_own.shape[0]
    return pl.pallas_call(
        mask_kernel,
        out_shape=(
            jax.ShapeDtypeStruct((4, 128, 128), jnp.int32),
            jax.ShapeDtypeStruct((owned * 128, 512), BF16),
            jax.ShapeDtypeStruct(own.shape, BF16),
        ),
        in_specs=[smem(), smem(), vmem(), vmem(), vmem(), vmem(), hbm()],
        out_specs=(vmem(), vmem(), vmem()),
        name="masks",
        cost_estimate=pl.CostEstimate(flops=1_000_000, bytes_accessed=2_000_000, transcendentals=0),
    )(groups, first, ids_wide, up_own, up_other, own, after)


def down_kernel(x_ref, own_ref, other_ref, code_ref, *rest):
    wide_ref, narrow_ref = rest[-2:]
    rows = x_ref.shape[0] * x_ref.shape[2]
    left = x_ref[:, 0].reshape(rows, x_ref.shape[3])
    right = x_ref[:, 1].reshape(rows, x_ref.shape[3])
    code = code_ref[...]
    total = jnp.zeros(wide_ref.shape, F32)
    for a in range(own_ref.shape[0]):
        product = jnp.dot(left, own_ref[a], preferred_element_type=F32)
        product = product + jnp.dot(right, other_ref[a], preferred_element_type=F32)
        total = jnp.where(code == a, product, total)
    wide_ref[...] = total
    narrow_ref[...] = total.astype(BF16)


def down_block(x, own, other, code, after=()):
    return pl.pallas_call(
        down_kernel,
        out_shape=(
            jax.ShapeDtypeStruct((128, 128), F32),
            jax.ShapeDtypeStruct((128, 128), BF16),
        ),
        in_specs=[vmem()] * 4 + [hbm()] * len(after),
        out_specs=(vmem(), vmem()),
        name="down",
        cost_estimate=pl.CostEstimate(
            flops=2 * 128 * 2048 * 512, bytes_accessed=1_000_000, transcendentals=0
        ),
    )(x, own, other, code, *after)


def up_kernel(t_ref, r0, r1, r2, r3, code_ref, up_ref, d0, d1, d2, d3, held):
    t = t_ref[0]
    for m, ref in enumerate((r0, r1, r2, r3)):
        held[m] = ref[...]
    for k2, out in enumerate((d0, d1, d2, d3)):
        low = held[jnp.bitwise_xor(t, k2)]
        code = code_ref[k2]
        zero = jnp.zeros_like(low)
        spread = jnp.concatenate(
            [jnp.where(code == a, low.astype(F32), 0.0).astype(BF16) for a in range(up_ref.shape[0] // 128)], 1
        )
        out[...] = jnp.dot(spread, up_ref[...], preferred_element_type=F32).astype(BF16)


def up_blocks(t, slots, code, up):
    return pl.pallas_call(
        up_kernel,
        out_shape=[jax.ShapeDtypeStruct((128, 512), BF16)] * 4,
        in_specs=[smem()] + [vmem()] * 6,
        out_specs=[vmem()] * 4,
        scratch_shapes=[pltpu.VMEM((4, 128, 128), BF16)],
        name="up",
        cost_estimate=pl.CostEstimate(
            flops=2 * 512 * 512 * 512, bytes_accessed=2_000_000, transcendentals=0
        ),
    )(t, *slots, code, up)


def attention_kernel(lengths_ref, q_ref, k_ref, v_ref, after_ref, top_ref, total_ref, sum_ref):
    step = pl.program_id(0)
    per = q_ref.shape[0]
    for n in range(per):
        length = lengths_ref[step * per + n]
        scores = lax.dot_general(
            q_ref[n], k_ref[n], (((1,), (1,)), ((), ())), preferred_element_type=F32
        ) * (1.0 / math.sqrt(HEAD_SIZE))
        spot = lax.broadcasted_iota(jnp.int32, scores.shape, 1)
        scores = jnp.where(spot < length, scores, -jnp.inf)
        top = jnp.max(scores, -1, keepdims=True)
        weight = jnp.exp(scores - top)
        total = jnp.sum(weight, -1, keepdims=True)
        top_ref[n] = jnp.broadcast_to(top, top_ref.shape[1:])
        total_ref[n] = jnp.broadcast_to(total, total_ref.shape[1:])
        sum_ref[n] = jnp.dot(weight.astype(BF16), v_ref[n], preferred_element_type=F32)


def cached_attention(lengths, queries, k_cache, value_cache, after):
    rows, context, _ = k_cache.shape
    heads = queries.shape[1]
    per = 4
    wide = jax.ShapeDtypeStruct((rows, heads, HEAD_SIZE), F32)
    block = lambda n: pl.BlockSpec((per, n, HEAD_SIZE), lambda i: (i, 0, 0))
    return pl.pallas_call(
        attention_kernel,
        grid=(rows // per,),
        out_shape=(wide, wide, wide),
        in_specs=[smem(), block(heads), block(context), block(context), hbm()],
        out_specs=(block(heads), block(heads), block(heads)),
        name="cached",
        cost_estimate=pl.CostEstimate(
            flops=4 * rows * heads * context * HEAD_SIZE,
            bytes_accessed=4 * rows * context * HEAD_SIZE,
            transcendentals=rows * heads * context,
        ),
    )(lengths, queries, k_cache, value_cache, after)


def base_kernel(j_ref, s0, s1, s2, s3, p_ref, o_ref, w_ref, out_ref, held):
    step = pl.program_id(0)

    @pl.when(step == 0)
    def _():
        for m, ref in enumerate((s0, s1, s2, s3)):
            held[2 * m] = ref[...]
            held[2 * m + 1] = p_ref[1] if m == 0 else o_ref[m - 1]
        out_ref[...] = jnp.zeros_like(out_ref)

    out_ref[...] += jnp.dot(
        held[jnp.bitwise_xor(j_ref[0], step)], w_ref[...], preferred_element_type=F32
    )


def base_projection(j, slots, pair, others, weight):
    group, width = slots[0].shape
    columns = weight.shape[1]
    whole = lambda x: pl.BlockSpec(x.shape, lambda i: (0,) * x.ndim)
    return pl.pallas_call(
        base_kernel,
        grid=(8,),
        out_shape=jax.ShapeDtypeStruct((group, columns), F32),
        in_specs=[smem()]
        + [whole(x) for x in (*slots, pair, others)]
        + [pl.BlockSpec((width, columns), lambda i: (i, 0))],
        out_specs=pl.BlockSpec((group, columns), lambda i: (0, 0)),
        scratch_shapes=[pltpu.VMEM((8, group, width), BF16)],
        name="base",
        cost_estimate=pl.CostEstimate(
            flops=2 * group * 8 * width * columns,
            bytes_accessed=2 * 8 * width * columns,
            transcendentals=0,
        ),
    )(j, *slots, pair, others, weight)


def final_kernel(
    base_ref, kept_ref, came_ref, cos_ref, sin_ref, q_ref, top_ref, total_ref, sum_ref,
    new_ref, out_ref, held, result,
):
    rows, queries, _ = q_ref.shape
    heads = queries // 2
    update = kept_ref[...].astype(F32) + came_ref[...].astype(F32)
    projected = base_ref[...] + update
    key = projected[:, :HEAD_SIZE]
    turned = pltpu.roll(key, HEAD_SIZE // 2, 1)
    key = key * cos_ref[...] + turned * sin_ref[...]
    fresh = jnp.concatenate([key, projected[:, HEAD_SIZE:]], 1).astype(BF16)
    held[0] = fresh[:, :HEAD_SIZE].astype(F32)
    held[1] = fresh[:, HEAD_SIZE:].astype(F32)
    q = q_ref[...].astype(F32)
    scale = 1.0 / math.sqrt(HEAD_SIZE)
    keys = [held[0, pl.ds(s, rows, stride=2), :] for s in range(2)]
    values = [held[1, pl.ds(s, rows, stride=2), :] for s in range(2)]
    scores = [jnp.sum(q * k[:, None, :], -1, keepdims=True) * scale for k in keys]
    second = lax.broadcasted_iota(jnp.int32, scores[1].shape, 1) >= heads
    scores[1] = jnp.where(second, scores[1], -jnp.inf)
    top = top_ref[...]
    highest = jnp.maximum(top, jnp.maximum(scores[0], scores[1]))
    old = jnp.exp(top - highest)
    new = [jnp.exp(s - highest) for s in scores]
    total = total_ref[...] * old + new[0] + new[1]
    mixed = sum_ref[...] * old + new[0] * values[0][:, None, :] + new[1] * values[1][:, None, :]
    result[...] = (mixed / total).reshape(rows * queries, HEAD_SIZE)
    new_ref[:, :, :HEAD_SIZE] = jnp.stack(keys, 1).astype(BF16)
    new_ref[:, :, HEAD_SIZE:] = jnp.stack(values, 1).astype(BF16)
    for g in range(heads):
        both = [result[pl.ds(s * heads + g, rows, stride=queries), :] for s in range(2)]
        out_ref[:, :, HEAD_SIZE * g : HEAD_SIZE * (g + 1)] = jnp.stack(both, 1).astype(BF16)


def final_merge(base, kept, came, cosine, sine, q, top, total, gathered):
    rows, queries, _ = q.shape
    group = 2 * rows
    return pl.pallas_call(
        final_kernel,
        out_shape=(
            jax.ShapeDtypeStruct((rows, 2, 2 * HEAD_SIZE), BF16),
            jax.ShapeDtypeStruct((rows, 2, queries // 2 * HEAD_SIZE), BF16),
        ),
        in_specs=[vmem()] * 9,
        out_specs=(vmem(), vmem()),
        scratch_shapes=[
            pltpu.VMEM((2, group, HEAD_SIZE), F32),
            pltpu.VMEM((rows * queries, HEAD_SIZE), F32),
        ],
        name="merge",
        cost_estimate=pl.CostEstimate(flops=2_000_000, bytes_accessed=1_000_000, transcendentals=1000),
    )(base, kept, came, cosine, sine, q, top, total, gathered)


def per_device(
    hidden_rows,
    key_value_weight,
    adapter_down_weight,
    adapter_up_weight,
    adapter_ids,
    kv_lengths,
    queries,
    k_cache,
    value_cache,
):
    rows, steps, width = hidden_rows.shape
    owned = adapter_down_weight.shape[0]
    group = rows * steps
    me = lax.axis_index("dp")
    j = lax.axis_index("tensor")
    t, c = j // 2, j % 2

    own = lax.optimization_barrier(hidden_rows.reshape(group, width))
    pair = jnp.stack([own, swap_core(own)])

    start = cross_z(pair)
    down_other = swap_core(adapter_down_weight)
    up_other = swap_core(adapter_up_weight)
    line = jnp.stack([start] + [first_axis(start, k) for k in (1, 2, 3)])
    blocks = {0: line}
    for k in (1, 3, 2):
        blocks[k] = second_axis(line, k)

    k2 = jnp.arange(4, dtype=jnp.int32)[:, None]
    k1 = jnp.arange(4, dtype=jnp.int32)[None, :]
    groups = me ^ (16 * c) ^ jnp.where(c == 0, 4 * k1 + k2, 4 * k2 + k1)
    ids_wide = jnp.broadcast_to(
        jnp.repeat(adapter_ids, steps).reshape(-1, group, 1), (32, group, 128)
    )
    code, up, same = make_masks(
        groups.reshape(16),
        (me * owned).reshape(1),
        ids_wide,
        adapter_up_weight,
        up_other,
        own,
        line,
    )

    q = queries.reshape(rows, -1, HEAD_SIZE)
    top, total, gathered = cached_attention(kv_lengths, q, k_cache, value_cache, line)
    chips = [same] + [along_z(same, m) for m in (1, 2, 3)]

    wide, narrow = [], []
    for k in range(4):
        after = (top, *chips[1:]) if k == 2 else ()
        w, n = down_block(blocks[k], adapter_down_weight, down_other, code[k], after)
        wide.append(w)
        narrow.append(n)
    wide, narrow = jnp.stack(wide), jnp.stack(narrow)

    mine = lax.dynamic_index_in_dim(wide, t, 0, keepdims=False)
    for m in (1, 2, 3):
        sent = lax.dynamic_index_in_dim(narrow, t ^ m, 0, keepdims=False)
        mine = mine + along_z(sent, m).astype(F32)
    mine = mine.astype(BF16)
    slots = [mine] + [along_z(mine, m) for m in (1, 2, 3)]
    delta = up_blocks(t.reshape(1), slots, code, up)

    back = delta[0]
    for k in (1, 3, 2):
        back = back + second_axis(delta[k], k)
    back = back.reshape(4, group, 4 * HEAD_SIZE)
    home = back[0]
    for k in (1, 3, 2):
        home = home + first_axis(back[k], k)
    here, there = home[:, : 2 * HEAD_SIZE], swap_core(home[:, 2 * HEAD_SIZE :])
    kept = jnp.where(c == 0, here, there)
    came = swap_z(jnp.where(c == 0, there, here))

    others = swap_core(jnp.stack(chips[1:]))
    base = base_projection(j.reshape(1), chips, pair, others, key_value_weight)

    half = HEAD_SIZE // 2
    frequency = jnp.exp(jnp.arange(half, dtype=F32) * (-2.0 * math.log(500000.0) / HEAD_SIZE))
    positions = (kv_lengths[:, None] + jnp.arange(steps, dtype=jnp.int32)[None, :]).reshape(group)
    angles = positions.astype(F32)[:, None] * frequency
    cosine, sine = jnp.cos(angles), jnp.sin(angles)
    cosine = jnp.concatenate([cosine, cosine], 1)
    sine = jnp.concatenate([-sine, sine], 1)
    return final_merge(base, kept, came, cosine, sine, q, top, total, gathered)


def solution(mesh):
    return jax.shard_map(
        per_device,
        mesh=mesh,
        in_specs=(
            P("dp", None, "tensor"),
            P(None, "tensor"),
            P("dp", "tensor", None),
            P("dp", None, "tensor"),
            P(),
            P("dp"),
            P("dp", None, "tensor"),
            P("dp", None, "tensor"),
            P("dp", None, "tensor"),
        ),
        out_specs=(P("dp", None, "tensor"), P("dp", None, "tensor")),
        check_vma=False,
    )
```

```python
import functools
import math

import jax
import jax.numpy as jnp
from jax import lax
from jax.experimental import pallas as pl
from jax.experimental.pallas import tpu as pltpu
from jax.sharding import PartitionSpec as P

HEAD_SIZE = 128
F32 = jnp.float32
BF16 = jnp.bfloat16
BOTH = ("dp", "tensor")


def pairs_of(move):
    pairs = []
    for d in range(32):
        for j in range(8):
            z, x, y, t, c = d // 16, d // 4 % 4, d % 4, j // 2, j % 2
            z, x, y, t, c = move(z, x, y, t, c)
            pairs.append((d * 8 + j, (z * 16 + x * 4 + y) * 8 + t * 2 + c))
    return pairs


def swap_core(value):
    return lax.ppermute(value, BOTH, pairs_of(lambda z, x, y, t, c: (z, x, y, t, c ^ 1)))


def cross_z(value):
    return lax.ppermute(value, BOTH, pairs_of(lambda z, x, y, t, c: (z ^ c, x, y, t, c)))


def first_axis(value, k):
    return lax.ppermute(
        value,
        BOTH,
        pairs_of(lambda z, x, y, t, c: (z, x ^ (0 if c else k), y ^ (k if c else 0), t, c)),
    )


def second_axis(value, k):
    return lax.ppermute(
        value,
        BOTH,
        pairs_of(lambda z, x, y, t, c: (z, x ^ (k if c else 0), y ^ (0 if c else k), t, c)),
    )


def along_x(value, k):
    return lax.ppermute(value, BOTH, pairs_of(lambda z, x, y, t, c: (z, x ^ (0 if c else k), y ^ (k if c else 0), t, c)))


def along_y(value, k):
    return lax.ppermute(value, BOTH, pairs_of(lambda z, x, y, t, c: (z, x ^ (k if c else 0), y ^ (0 if c else k), t, c)))


def along_z(value, k):
    return lax.ppermute(value, BOTH, pairs_of(lambda z, x, y, t, c: (z, x, y, t ^ k, c)))


def swap_z(value):
    return lax.ppermute(value, BOTH, pairs_of(lambda z, x, y, t, c: (z ^ 1, x, y, t, c)))


def anywhere():
    return pl.BlockSpec(memory_space=pl.ANY)


def hbm():
    return pl.BlockSpec(memory_space=pltpu.HBM)


def vmem():
    return pl.BlockSpec(memory_space=pltpu.VMEM)


def smem():
    return pl.BlockSpec(memory_space=pltpu.SMEM)


def limit(mebibytes):
    return pltpu.CompilerParams(vmem_limit_bytes=mebibytes << 20)


def small(name, kernel, out_shape, in_specs, args, mebibytes=2, scratch=()):
    many = isinstance(out_shape, (list, tuple))
    return pl.pallas_call(
        kernel,
        out_shape=out_shape,
        in_specs=in_specs,
        out_specs=[vmem()] * len(out_shape) if many else vmem(),
        scratch_shapes=scratch,
        name=name,
        compiler_params=limit(mebibytes),
        cost_estimate=pl.CostEstimate(flops=100_000, bytes_accessed=200_000, transcendentals=0),
    )(*args)


def stack_kernel(*refs):
    for n in range(refs[-1].shape[0]):
        refs[-1][n] = refs[n][...]


def stack(*parts, after=None):
    shape = jax.ShapeDtypeStruct((len(parts), *parts[0].shape), parts[0].dtype)
    specs = [vmem()] * len(parts)
    if after is not None:
        parts, specs = (*parts, after), [*specs, anywhere()]
    return small("stack", stack_kernel, shape, specs, parts)


def line_kernel(a_ref, b_ref, c_ref, d_ref, low_ref, high_ref):
    low_ref[0] = a_ref[...]
    low_ref[1] = b_ref[...]
    high_ref[0] = c_ref[...]
    high_ref[1] = d_ref[...]


def line_halves(*parts):
    shape = jax.ShapeDtypeStruct((2, *parts[0].shape), parts[0].dtype)
    return small("line", line_kernel, (shape, shape), [vmem()] * 4, parts, 3)


def pack_kernel(n_ref, *refs):
    out_ref = refs[-1]
    for m in range(4):
        out_ref[2 * m : 2 * m + 2] = refs[m][...]
        out_ref[8 + m] = n_ref[0] if m == 0 else refs[3 + m][1]


def pack(chunks, *parts):
    shape = jax.ShapeDtypeStruct((12, *parts[0].shape[1:]), parts[0].dtype)
    return small("pack", pack_kernel, shape, [vmem()] * 8, (chunks, *parts))


def query_kernel(lengths_ref, q_ref, after_ref, out_ref, bias_ref):
    out_ref[...] = q_ref[...]
    spot = lax.broadcasted_iota(jnp.int32, (1, bias_ref.shape[1]), 1)
    for r in range(bias_ref.shape[0]):
        bias_ref[r : r + 1, :] = jnp.where(spot < lengths_ref[r], 0.0, -jnp.inf)


def ready_queries(lengths, q, context, after):
    shapes = (
        jax.ShapeDtypeStruct(q.shape, q.dtype),
        jax.ShapeDtypeStruct((q.shape[0], context), F32),
    )
    return small("query", query_kernel, shapes, [smem(), vmem(), vmem()], (lengths, q, after))


def chunk_kernel(own_ref, after_ref, *out_refs):
    for h, out_ref in enumerate(out_refs):
        for i in range(4):
            at = h * 512 + i * 128
            out_ref[0, 32 * i : 32 * i + 32, :] = own_ref[:, at : at + 128]


def make_chunks(own, after):
    shapes = (jax.ShapeDtypeStruct((1, 128, 128), BF16),) * 2
    return small("chunks", chunk_kernel, shapes, [vmem(), vmem()], (own, after))


def wide_kernel(up_ref, after_ref, wide_ref):
    wide_ref[...] = jnp.zeros_like(wide_ref)
    for a in range(up_ref.shape[0]):
        wide_ref[128 * a : 128 * a + 64, :128] = up_ref[a, :, :128]
        wide_ref[128 * a + 64 : 128 * a + 128, 128:] = up_ref[a, :, 128:]


def widen(up, after):
    shape = jax.ShapeDtypeStruct((up.shape[0] * 128, 256), BF16)
    return small("widen", wide_kernel, shape, [vmem(), vmem()], (up, after))


def code_kernel(groups_ref, first_ref, ids_ref, after_ref, out_ref, held):
    rows = ids_ref.shape[1]
    place = lax.broadcasted_iota(jnp.int32, (rows, 2 * rows), 1) // 2
    twice = (place == lax.broadcasted_iota(jnp.int32, (rows, 2 * rows), 0)).astype(BF16)
    ids = ids_ref[...].astype(F32).astype(BF16)
    held[...] = jnp.dot(ids, twice, preferred_element_type=F32) - first_ref[0].astype(F32)
    for n in range(out_ref.shape[0]):
        picked = [held[pl.ds(groups_ref[4 * n + k], 1), :] for k in range(4)]
        out_ref[n : n + 1, :] = jnp.concatenate(picked, 1)


def make_codes(groups, first, ids, after):
    return pl.pallas_call(
        code_kernel,
        out_shape=jax.ShapeDtypeStruct((8, 128), F32),
        in_specs=[smem(), smem(), vmem(), vmem()],
        out_specs=vmem(),
        scratch_shapes=[pltpu.VMEM((ids.shape[0], 2 * ids.shape[1]), F32)],
        name="codes",
        compiler_params=limit(1),
        cost_estimate=pl.CostEstimate(flops=100_000, bytes_accessed=100_000, transcendentals=0),
    )(groups, first, ids, after)


def column(codes_ref, n):
    return jnp.broadcast_to(codes_ref[n : n + 1, :], (128, 128)).T


def down_kernel(block, low_ref, high_ref, own_ref, other_ref, codes_ref, *rest):
    out_ref = rest[-1]
    half = low_ref.shape[0] * low_ref.shape[2]
    sides = [
        jnp.concatenate([ref[:, n].reshape(half, ref.shape[3]) for ref in (low_ref, high_ref)], 0)
        for n in range(2)
    ]
    code = column(codes_ref, block)
    total = jnp.zeros(out_ref.shape, F32)
    for a in range(own_ref.shape[0]):
        product = jnp.dot(sides[0], own_ref[a], preferred_element_type=F32)
        product = product + jnp.dot(sides[1], other_ref[a], preferred_element_type=F32)
        total = jnp.where(code == a, product, total)
    out_ref[...] = total.astype(BF16)


def down_block(block, halves, own, other, codes, after=()):
    return pl.pallas_call(
        functools.partial(down_kernel, block),
        out_shape=jax.ShapeDtypeStruct((128, 128), BF16),
        in_specs=[vmem()] * 5 + [anywhere()] * len(after),
        out_specs=vmem(),
        name="down",
        compiler_params=limit(6),
        cost_estimate=pl.CostEstimate(
            flops=2 * 128 * 2048 * 512, bytes_accessed=1_000_000, transcendentals=0
        ),
    )(*halves, own, other, codes, *after)


def up_kernel(t_ref, r0, r1, r2, r3, other_ref, codes_ref, wide_ref, d0, d1, d2, d3, held):
    t = t_ref[0]
    outs = (d0, d1, d2, d3)
    for m, ref in enumerate((r0, r1, r2, r3)):
        held[m] = ref[0]

    def grown(low, code):
        low = low.astype(F32)
        spread = jnp.concatenate(
            [jnp.where(code == a, low, 0.0).astype(BF16) for a in range(wide_ref.shape[0] // 128)],
            1,
        )
        return jnp.dot(spread, wide_ref[...], preferred_element_type=F32).astype(BF16)

    for k2 in range(4):
        block = grown(held[jnp.bitwise_xor(t, k2)], column(codes_ref, k2))
        outs[k2][:, 0] = block.reshape(4, 32, 256)
        block = grown(other_ref[2 * jnp.bitwise_xor(t, k2)], column(codes_ref, 4 + k2))
        for k1 in range(4):
            outs[k1][k2, 1] = block[32 * k1 : 32 * k1 + 32]


def up_blocks(t, slots, others, codes, wide):
    return pl.pallas_call(
        up_kernel,
        out_shape=[jax.ShapeDtypeStruct((4, 2, 32, 256), BF16)] * 4,
        in_specs=[smem()] + [vmem()] * 7,
        out_specs=[vmem()] * 4,
        scratch_shapes=[pltpu.VMEM((4, 128, 128), BF16)],
        name="up",
        compiler_params=limit(4),
        cost_estimate=pl.CostEstimate(
            flops=2 * 1024 * 512 * 256, bytes_accessed=2_000_000, transcendentals=0
        ),
    )(t, *slots, others, codes, wide)


def cached_attention(queries, bias, k_cache, value_cache):
    scores = jnp.einsum("rqd,rjd->rqj", queries, k_cache, preferred_element_type=F32)
    scores = scores * (1.0 / math.sqrt(HEAD_SIZE)) + bias[:, None, :]
    top = jnp.max(scores, -1, keepdims=True)
    weight = jnp.exp(scores - top)
    total = jnp.sum(weight, -1, keepdims=True)
    gathered = jnp.einsum(
        "rqj,rjd->rqd", weight.astype(BF16), value_cache, preferred_element_type=F32
    )
    wide = lambda x: jnp.broadcast_to(x, gathered.shape)
    return wide(top), wide(total), gathered


def row_kernel(j_ref, n0, n1, r1, r2, r3, g1, g2, g3, others_ref, out_ref, held):
    own = ((n0, n1), (r1, g1), (r2, g2), (r3, g3))
    for m in range(4):
        for h in range(2):
            held[2 * m, h] = own[m][h][0 if m == 0 else 1]
            held[2 * m + 1, h] = others_ref[2 * m + 1 if h else 8 + m]
    for n in range(8):
        for h in range(2):
            chunk = held[jnp.bitwise_xor(j_ref[0], n), h]
            for i in range(4):
                at = n * 1024 + h * 512 + i * 128
                out_ref[:, at : at + 128] = chunk[32 * i : 32 * i + 32, :]


def whole_rows(j, chunks, scattered, gathered, others):
    return pl.pallas_call(
        row_kernel,
        out_shape=jax.ShapeDtypeStruct((32, 8192), BF16),
        in_specs=[smem()] + [vmem()] * 9,
        out_specs=vmem(),
        scratch_shapes=[pltpu.VMEM((8, 2, 128, 128), BF16)],
        name="rows",
        compiler_params=limit(3),
        cost_estimate=pl.CostEstimate(flops=0, bytes_accessed=1_000_000, transcendentals=0),
    )(j, *chunks, *scattered, *gathered, others)


def split_kernel(c_ref, home_ref, after_ref, kept_ref, sent_ref):
    kept_ref[...] = home_ref[c_ref[0]]
    sent_ref[...] = home_ref[1 - c_ref[0]]


def final_kernel(
    base_ref, kept_ref, came_ref, cos_ref, sin_ref, q_ref, top_ref, total_ref, sum_ref,
    new_ref, out_ref, held, result,
):
    rows, queries, _ = q_ref.shape
    heads = queries // 2
    update = kept_ref[...].astype(F32) + came_ref[...].astype(F32)
    projected = base_ref[...] + update
    key = projected[:, :HEAD_SIZE]
    turned = pltpu.roll(key, HEAD_SIZE // 2, 1)
    key = key * cos_ref[...] + turned * sin_ref[...]
    fresh = jnp.concatenate([key, projected[:, HEAD_SIZE:]], 1).astype(BF16)
    held[0] = fresh[:, :HEAD_SIZE].astype(F32)
    held[1] = fresh[:, HEAD_SIZE:].astype(F32)
    q = q_ref[...].astype(F32)
    scale = 1.0 / math.sqrt(HEAD_SIZE)
    keys = [held[0, pl.ds(s, rows, stride=2), :] for s in range(2)]
    values = [held[1, pl.ds(s, rows, stride=2), :] for s in range(2)]
    scores = [jnp.sum(q * k[:, None, :], -1, keepdims=True) * scale for k in keys]
    second = lax.broadcasted_iota(jnp.int32, scores[1].shape, 1) >= heads
    scores[1] = jnp.where(second, scores[1], -jnp.inf)
    top = top_ref[...]
    highest = jnp.maximum(top, jnp.maximum(scores[0], scores[1]))
    old = jnp.exp(top - highest)
    new = [jnp.exp(s - highest) for s in scores]
    total = total_ref[...] * old + new[0] + new[1]
    mixed = sum_ref[...] * old + new[0] * values[0][:, None, :] + new[1] * values[1][:, None, :]
    result[...] = (mixed / total).reshape(rows * queries, HEAD_SIZE)
    new_ref[:, :, :HEAD_SIZE] = jnp.stack(keys, 1).astype(BF16)
    new_ref[:, :, HEAD_SIZE:] = jnp.stack(values, 1).astype(BF16)
    for g in range(heads):
        both = [result[pl.ds(s * heads + g, rows, stride=queries), :] for s in range(2)]
        out_ref[:, :, HEAD_SIZE * g : HEAD_SIZE * (g + 1)] = jnp.stack(both, 1).astype(BF16)


def final_merge(base, kept, came, cosine, sine, q, top, total, gathered):
    rows, queries, _ = q.shape
    group = 2 * rows
    return pl.pallas_call(
        final_kernel,
        out_shape=(
            jax.ShapeDtypeStruct((rows, 2, 2 * HEAD_SIZE), BF16),
            jax.ShapeDtypeStruct((rows, 2, queries // 2 * HEAD_SIZE), BF16),
        ),
        in_specs=[vmem()] * 9,
        out_specs=(vmem(), vmem()),
        scratch_shapes=[
            pltpu.VMEM((2, group, HEAD_SIZE), F32),
            pltpu.VMEM((rows * queries, HEAD_SIZE), F32),
        ],
        name="merge",
        compiler_params=limit(6),
        cost_estimate=pl.CostEstimate(flops=2_000_000, bytes_accessed=1_000_000, transcendentals=1000),
    )(base, kept, came, cosine, sine, q, top, total, gathered)


def per_device(
    hidden_rows,
    key_value_weight,
    adapter_down_weight,
    adapter_up_weight,
    adapter_ids,
    kv_lengths,
    queries,
    k_cache,
    value_cache,
):
    rows, steps, width = hidden_rows.shape
    owned = adapter_down_weight.shape[0]
    group = rows * steps
    me = lax.axis_index("dp")
    j = lax.axis_index("tensor")
    t, c = j // 2, j % 2

    own = lax.optimization_barrier(hidden_rows.reshape(group, width))
    pair = stack(own, swap_core(own))
    down_other = swap_core(adapter_down_weight)

    k2 = jnp.arange(4, dtype=jnp.int32)[:, None]
    k1 = jnp.arange(4, dtype=jnp.int32)[None, :]
    blocks_of = lambda core: (
        me ^ (16 * core) ^ jnp.where(core == 0, 4 * k1 + k2, 4 * k2 + k1)
    ).reshape(16)
    groups = jnp.concatenate([blocks_of(c), blocks_of(1 - c)])

    start = cross_z(pair)
    low, high = line_halves(start, *[along_x(start, k) for k in (1, 2, 3)])
    low3, high1 = along_y(low, 3), along_y(high, 1)
    q = queries.reshape(rows, -1, HEAD_SIZE)
    top, total, gathered = cached_attention(
        *ready_queries(kv_lengths, q, k_cache.shape[1], start), k_cache, value_cache
    )
    high3, low1 = along_y(high, 3), along_y(low, 1)
    low2, high2 = along_y(low3, 1), along_y(high1, 3)
    blocks = ((low, high), (low1, high1), (low2, high2), (low3, high3))

    codes = make_codes(groups, (me * owned).reshape(1), adapter_ids.reshape(-1, rows), start)
    partial = []
    for k in range(4):
        after = (gathered,) if k == 2 else ()
        partial.append(
            down_block(k, blocks[k], adapter_down_weight, down_other, codes, after)
        )
    partial = jnp.stack(partial)

    chunks = make_chunks(own, low)
    mine = lax.dynamic_index_in_dim(partial, t, 0, keepdims=False).astype(F32)
    came = []
    for m in (1, 2, 3):
        sent = lax.dynamic_index_in_dim(partial, t ^ m, 0, keepdims=False)
        came.append(along_z(jnp.stack([sent, chunks[0][0]]), m))
        mine = mine + came[-1][0].astype(F32)
    both = jnp.stack([mine.astype(BF16), chunks[1][0]])
    slots = [along_z(both, m) for m in (1, 2, 3)]
    wide = widen(adapter_up_weight, both)
    others = swap_core(pack(chunks[0], both, *slots, *came))
    delta = up_blocks(jnp.stack([t, c]), (both, *slots), others, codes, wide)
    full = whole_rows(j.reshape(1), chunks, came, slots, others)

    back = delta[0]
    for k in (1, 3, 2):
        back = back + second_axis(delta[k], k)
    home = back[0]
    for k in (1, 3, 2):
        home = home + first_axis(back[k], k)
    half = full.shape[1] // 2
    base = jnp.dot(full[:, :half], key_value_weight[:half], preferred_element_type=F32)
    kept, sent = small(
        "split",
        split_kernel,
        (jax.ShapeDtypeStruct(home.shape[1:], BF16),) * 2,
        [smem(), vmem(), vmem()],
        (c.reshape(1), home, base),
    )
    came = swap_z(sent)
    base = base + jnp.dot(full[:, half:], key_value_weight[half:], preferred_element_type=F32)

    half = HEAD_SIZE // 2
    frequency = jnp.exp(jnp.arange(half, dtype=F32) * (-2.0 * math.log(500000.0) / HEAD_SIZE))
    positions = (kv_lengths[:, None] + jnp.arange(steps, dtype=jnp.int32)[None, :]).reshape(group)
    angles = positions.astype(F32)[:, None] * frequency
    cosine, sine = jnp.cos(angles), jnp.sin(angles)
    cosine = jnp.concatenate([cosine, cosine], 1)
    sine = jnp.concatenate([-sine, sine], 1)
    return final_merge(base, kept, came, cosine, sine, q, top, total, gathered)


def solution(mesh):
    return jax.shard_map(
        per_device,
        mesh=mesh,
        in_specs=(
            P("dp", None, "tensor"),
            P(None, "tensor"),
            P("dp", "tensor", None),
            P("dp", None, "tensor"),
            P(),
            P("dp"),
            P("dp", None, "tensor"),
            P("dp", None, "tensor"),
            P("dp", None, "tensor"),
        ),
        out_specs=(P("dp", None, "tensor"), P("dp", None, "tensor")),
        check_vma=False,
    )
```

```python
import functools
import math

import jax
import jax.numpy as jnp
from jax import lax
from jax.experimental import pallas as pl
from jax.experimental.pallas import tpu as pltpu
from jax.sharding import PartitionSpec as P

HEAD_SIZE = 128
F32 = jnp.float32
BF16 = jnp.bfloat16
BOTH = ("dp", "tensor")


def pairs_of(move):
    pairs = []
    for d in range(32):
        for j in range(8):
            z, x, y, t, c = d // 16, d // 4 % 4, d % 4, j // 2, j % 2
            z, x, y, t, c = move(z, x, y, t, c)
            pairs.append((d * 8 + j, (z * 16 + x * 4 + y) * 8 + t * 2 + c))
    return pairs


def swap_core(value):
    return lax.ppermute(value, BOTH, pairs_of(lambda z, x, y, t, c: (z, x, y, t, c ^ 1)))


def cross_z(value):
    return lax.ppermute(value, BOTH, pairs_of(lambda z, x, y, t, c: (z ^ c, x, y, t, c)))


def first_axis(value, k):
    return lax.ppermute(
        value,
        BOTH,
        pairs_of(lambda z, x, y, t, c: (z, x ^ (0 if c else k), y ^ (k if c else 0), t, c)),
    )


def second_axis(value, k):
    return lax.ppermute(
        value,
        BOTH,
        pairs_of(lambda z, x, y, t, c: (z, x ^ (k if c else 0), y ^ (0 if c else k), t, c)),
    )


def along_x(value, k):
    return lax.ppermute(value, BOTH, pairs_of(lambda z, x, y, t, c: (z, x ^ (0 if c else k), y ^ (k if c else 0), t, c)))


def along_y(value, k):
    return lax.ppermute(value, BOTH, pairs_of(lambda z, x, y, t, c: (z, x ^ (k if c else 0), y ^ (0 if c else k), t, c)))


def along_z(value, k):
    return lax.ppermute(value, BOTH, pairs_of(lambda z, x, y, t, c: (z, x, y, t ^ k, c)))


def swap_z(value):
    return lax.ppermute(value, BOTH, pairs_of(lambda z, x, y, t, c: (z ^ 1, x, y, t, c)))


def anywhere():
    return pl.BlockSpec(memory_space=pl.ANY)


def hbm():
    return pl.BlockSpec(memory_space=pltpu.HBM)


def vmem():
    return pl.BlockSpec(memory_space=pltpu.VMEM)


def smem():
    return pl.BlockSpec(memory_space=pltpu.SMEM)


def limit(mebibytes):
    return pltpu.CompilerParams(vmem_limit_bytes=mebibytes << 20)


def small(name, kernel, out_shape, in_specs, args, mebibytes=2, scratch=()):
    many = isinstance(out_shape, (list, tuple))
    return pl.pallas_call(
        kernel,
        out_shape=out_shape,
        in_specs=in_specs,
        out_specs=[vmem()] * len(out_shape) if many else vmem(),
        scratch_shapes=scratch,
        name=name,
        compiler_params=limit(mebibytes),
        cost_estimate=pl.CostEstimate(flops=100_000, bytes_accessed=200_000, transcendentals=0),
    )(*args)


def flat_kernel(raw_ref, out_ref):
    out_ref[...] = raw_ref[...].reshape(out_ref.shape)


def flat_rows(raw):
    shape = jax.ShapeDtypeStruct((raw.shape[0] * raw.shape[1], raw.shape[2]), BF16)
    return small("flat", flat_kernel, shape, [vmem()], (raw,))


def rows_kernel(own_ref, other_ref, out_ref):
    out_ref[0] = own_ref[...]
    out_ref[1] = other_ref[...].reshape(out_ref.shape[1:])


def rows_of(own, other):
    shape = jax.ShapeDtypeStruct((2, *own.shape), BF16)
    return small("pair", rows_kernel, shape, [vmem()] * 2, (own, other))


def stack_kernel(*refs):
    for n in range(refs[-1].shape[0]):
        refs[-1][n] = refs[n][...]


def stack(*parts, after=None):
    shape = jax.ShapeDtypeStruct((len(parts), *parts[0].shape), parts[0].dtype)
    specs = [vmem()] * len(parts)
    if after is not None:
        parts, specs = (*parts, after), [*specs, anywhere()]
    return small("stack", stack_kernel, shape, specs, parts)


def line_kernel(a_ref, b_ref, c_ref, d_ref, low_ref, high_ref):
    low_ref[0] = a_ref[...]
    low_ref[1] = b_ref[...]
    high_ref[0] = c_ref[...]
    high_ref[1] = d_ref[...]


def line_halves(*parts):
    shape = jax.ShapeDtypeStruct((2, *parts[0].shape), parts[0].dtype)
    return small("line", line_kernel, (shape, shape), [vmem()] * 4, parts, 3)


def pack_kernel(n_ref, *refs):
    out_ref = refs[-1]
    for m in range(4):
        out_ref[2 * m : 2 * m + 2] = refs[m][...]
        out_ref[8 + m] = n_ref[0] if m == 0 else refs[3 + m][1]


def pack(chunks, *parts):
    shape = jax.ShapeDtypeStruct((12, *parts[0].shape[1:]), parts[0].dtype)
    return small("pack", pack_kernel, shape, [vmem()] * 8, (chunks, *parts))


def query_kernel(lengths_ref, q_ref, after_ref, out_ref, bias_ref):
    out_ref[...] = q_ref[...]
    spot = lax.broadcasted_iota(jnp.int32, (1, bias_ref.shape[1]), 1)
    for r in range(bias_ref.shape[0]):
        bias_ref[r : r + 1, :] = jnp.where(spot < lengths_ref[r], 0.0, -jnp.inf)


def ready_queries(lengths, q, context, after):
    shapes = (
        jax.ShapeDtypeStruct(q.shape, q.dtype),
        jax.ShapeDtypeStruct((q.shape[0], context), F32),
    )
    return small("query", query_kernel, shapes, [smem(), vmem(), vmem()], (lengths, q, after))


def chunk_kernel(own_ref, after_ref, *out_refs):
    for h, out_ref in enumerate(out_refs):
        for i in range(4):
            at = h * 512 + i * 128
            out_ref[0, 32 * i : 32 * i + 32, :] = own_ref[:, at : at + 128]


def make_chunks(own, after):
    shapes = (jax.ShapeDtypeStruct((1, 128, 128), BF16),) * 2
    return small("chunks", chunk_kernel, shapes, [vmem(), vmem()], (own, after))


def wide_kernel(up_ref, after_ref, wide_ref):
    wide_ref[...] = jnp.zeros_like(wide_ref)
    for a in range(up_ref.shape[0]):
        wide_ref[128 * a : 128 * a + 64, :128] = up_ref[a, :, :128]
        wide_ref[128 * a + 64 : 128 * a + 128, 128:] = up_ref[a, :, 128:]


def widen(up, after):
    shape = jax.ShapeDtypeStruct((up.shape[0] * 128, 256), BF16)
    return small("widen", wide_kernel, shape, [vmem(), vmem()], (up, after))


def code_kernel(groups_ref, first_ref, ids_ref, after_ref, out_ref, held):
    rows = ids_ref.shape[1]
    place = lax.broadcasted_iota(jnp.int32, (rows, 2 * rows), 1) // 2
    twice = (place == lax.broadcasted_iota(jnp.int32, (rows, 2 * rows), 0)).astype(BF16)
    ids = ids_ref[...].astype(F32).astype(BF16)
    held[...] = jnp.dot(ids, twice, preferred_element_type=F32) - first_ref[0].astype(F32)
    for n in range(out_ref.shape[0]):
        picked = [held[pl.ds(groups_ref[4 * n + k], 1), :] for k in range(4)]
        out_ref[n : n + 1, :] = jnp.concatenate(picked, 1)


def make_codes(groups, first, ids, after):
    return pl.pallas_call(
        code_kernel,
        out_shape=jax.ShapeDtypeStruct((8, 128), F32),
        in_specs=[smem(), smem(), vmem(), vmem()],
        out_specs=vmem(),
        scratch_shapes=[pltpu.VMEM((ids.shape[0], 2 * ids.shape[1]), F32)],
        name="codes",
        compiler_params=limit(1),
        cost_estimate=pl.CostEstimate(flops=100_000, bytes_accessed=100_000, transcendentals=0),
    )(groups, first, ids, after)


def column(codes_ref, n):
    return jnp.broadcast_to(codes_ref[n : n + 1, :], (128, 128)).T


def down_kernel(block, low_ref, high_ref, own_ref, other_ref, codes_ref, *rest):
    out_ref = rest[-1]
    half = low_ref.shape[0] * low_ref.shape[2]
    sides = [
        jnp.concatenate([ref[:, n].reshape(half, ref.shape[3]) for ref in (low_ref, high_ref)], 0)
        for n in range(2)
    ]
    code = column(codes_ref, block)
    total = jnp.zeros(out_ref.shape, F32)
    for a in range(own_ref.shape[0]):
        product = jnp.dot(sides[0], own_ref[a], preferred_element_type=F32)
        product = product + jnp.dot(sides[1], other_ref[a], preferred_element_type=F32)
        total = jnp.where(code == a, product, total)
    out_ref[...] = total.astype(BF16)


def down_block(block, halves, own, other, codes, after=()):
    return pl.pallas_call(
        functools.partial(down_kernel, block),
        out_shape=jax.ShapeDtypeStruct((128, 128), BF16),
        in_specs=[vmem()] * 5 + [anywhere()] * len(after),
        out_specs=vmem(),
        name="down",
        compiler_params=limit(6),
        cost_estimate=pl.CostEstimate(
            flops=2 * 128 * 2048 * 512, bytes_accessed=1_000_000, transcendentals=0
        ),
    )(*halves, own, other, codes, *after)


def up_kernel(t_ref, r0, r1, r2, r3, other_ref, codes_ref, wide_ref, d0, d1, d2, d3, held):
    t = t_ref[0]
    outs = (d0, d1, d2, d3)
    for m, ref in enumerate((r0, r1, r2, r3)):
        held[m] = ref[0]

    def grown(low, code):
        low = low.astype(F32)
        spread = jnp.concatenate(
            [jnp.where(code == a, low, 0.0).astype(BF16) for a in range(wide_ref.shape[0] // 128)],
            1,
        )
        return jnp.dot(spread, wide_ref[...], preferred_element_type=F32).astype(BF16)

    for k2 in range(4):
        block = grown(held[jnp.bitwise_xor(t, k2)], column(codes_ref, k2))
        outs[k2][:, 0] = block.reshape(4, 32, 256)
        block = grown(other_ref[2 * jnp.bitwise_xor(t, k2)], column(codes_ref, 4 + k2))
        for k1 in range(4):
            outs[k1][k2, 1] = block[32 * k1 : 32 * k1 + 32]


def up_blocks(t, slots, others, codes, wide):
    return pl.pallas_call(
        up_kernel,
        out_shape=[jax.ShapeDtypeStruct((4, 2, 32, 256), BF16)] * 4,
        in_specs=[smem()] + [vmem()] * 7,
        out_specs=[vmem()] * 4,
        scratch_shapes=[pltpu.VMEM((4, 128, 128), BF16)],
        name="up",
        compiler_params=limit(4),
        cost_estimate=pl.CostEstimate(
            flops=2 * 1024 * 512 * 256, bytes_accessed=2_000_000, transcendentals=0
        ),
    )(t, *slots, others, codes, wide)


def cached_attention(queries, bias, k_cache, value_cache):
    scores = jnp.einsum("rqd,rjd->rqj", queries, k_cache, preferred_element_type=F32)
    scores = scores * (1.0 / math.sqrt(HEAD_SIZE)) + bias[:, None, :]
    top = jnp.max(scores, -1, keepdims=True)
    weight = jnp.exp(scores - top)
    total = jnp.sum(weight, -1, keepdims=True)
    gathered = jnp.einsum(
        "rqj,rjd->rqd", weight.astype(BF16), value_cache, preferred_element_type=F32
    )
    wide = lambda x: jnp.broadcast_to(x, gathered.shape)
    return wide(top), wide(total), gathered


def row_kernel(j_ref, n0, n1, r1, r2, r3, g1, g2, g3, others_ref, out_ref, held):
    own = ((n0, n1), (r1, g1), (r2, g2), (r3, g3))
    for m in range(4):
        for h in range(2):
            held[2 * m, h] = own[m][h][0 if m == 0 else 1]
            held[2 * m + 1, h] = others_ref[2 * m + 1 if h else 8 + m]
    for n in range(8):
        for h in range(2):
            chunk = held[jnp.bitwise_xor(j_ref[0], n), h]
            for i in range(4):
                at = n * 1024 + h * 512 + i * 128
                out_ref[:, at : at + 128] = chunk[32 * i : 32 * i + 32, :]


def whole_rows(j, chunks, scattered, gathered, others):
    return pl.pallas_call(
        row_kernel,
        out_shape=jax.ShapeDtypeStruct((32, 8192), BF16),
        in_specs=[smem()] + [vmem()] * 9,
        out_specs=vmem(),
        scratch_shapes=[pltpu.VMEM((8, 2, 128, 128), BF16)],
        name="rows",
        compiler_params=limit(3),
        cost_estimate=pl.CostEstimate(flops=0, bytes_accessed=1_000_000, transcendentals=0),
    )(j, *chunks, *scattered, *gathered, others)


def split_kernel(c_ref, home_ref, after_ref, kept_ref, sent_ref):
    kept_ref[...] = home_ref[c_ref[0]]
    sent_ref[...] = home_ref[1 - c_ref[0]]


def final_kernel(
    base_ref, kept_ref, came_ref, cos_ref, sin_ref, q_ref, top_ref, total_ref, sum_ref,
    new_ref, out_ref, held, result,
):
    rows, queries, _ = q_ref.shape
    heads = queries // 2
    update = kept_ref[...].astype(F32) + came_ref[...].astype(F32)
    projected = base_ref[...] + update
    key = projected[:, :HEAD_SIZE]
    turned = pltpu.roll(key, HEAD_SIZE // 2, 1)
    key = key * cos_ref[...] + turned * sin_ref[...]
    fresh = jnp.concatenate([key, projected[:, HEAD_SIZE:]], 1).astype(BF16)
    held[0] = fresh[:, :HEAD_SIZE].astype(F32)
    held[1] = fresh[:, HEAD_SIZE:].astype(F32)
    q = q_ref[...].astype(F32)
    scale = 1.0 / math.sqrt(HEAD_SIZE)
    keys = [held[0, pl.ds(s, rows, stride=2), :] for s in range(2)]
    values = [held[1, pl.ds(s, rows, stride=2), :] for s in range(2)]
    scores = [jnp.sum(q * k[:, None, :], -1, keepdims=True) * scale for k in keys]
    second = lax.broadcasted_iota(jnp.int32, scores[1].shape, 1) >= heads
    scores[1] = jnp.where(second, scores[1], -jnp.inf)
    top = top_ref[...]
    highest = jnp.maximum(top, jnp.maximum(scores[0], scores[1]))
    old = jnp.exp(top - highest)
    new = [jnp.exp(s - highest) for s in scores]
    total = total_ref[...] * old + new[0] + new[1]
    mixed = sum_ref[...] * old + new[0] * values[0][:, None, :] + new[1] * values[1][:, None, :]
    result[...] = (mixed / total).reshape(rows * queries, HEAD_SIZE)
    new_ref[:, :, :HEAD_SIZE] = jnp.stack(keys, 1).astype(BF16)
    new_ref[:, :, HEAD_SIZE:] = jnp.stack(values, 1).astype(BF16)
    for g in range(heads):
        both = [result[pl.ds(s * heads + g, rows, stride=queries), :] for s in range(2)]
        out_ref[:, :, HEAD_SIZE * g : HEAD_SIZE * (g + 1)] = jnp.stack(both, 1).astype(BF16)


def final_merge(base, kept, came, cosine, sine, q, top, total, gathered):
    rows, queries, _ = q.shape
    group = 2 * rows
    return pl.pallas_call(
        final_kernel,
        out_shape=(
            jax.ShapeDtypeStruct((rows, 2, 2 * HEAD_SIZE), BF16),
            jax.ShapeDtypeStruct((rows, 2, queries // 2 * HEAD_SIZE), BF16),
        ),
        in_specs=[vmem()] * 9,
        out_specs=(vmem(), vmem()),
        scratch_shapes=[
            pltpu.VMEM((2, group, HEAD_SIZE), F32),
            pltpu.VMEM((rows * queries, HEAD_SIZE), F32),
        ],
        name="merge",
        compiler_params=limit(6),
        cost_estimate=pl.CostEstimate(flops=2_000_000, bytes_accessed=1_000_000, transcendentals=1000),
    )(base, kept, came, cosine, sine, q, top, total, gathered)


def per_device(
    hidden_rows,
    key_value_weight,
    adapter_down_weight,
    adapter_up_weight,
    adapter_ids,
    kv_lengths,
    queries,
    k_cache,
    value_cache,
):
    rows, steps, width = hidden_rows.shape
    owned = adapter_down_weight.shape[0]
    group = rows * steps
    me = lax.axis_index("dp")
    j = lax.axis_index("tensor")
    t, c = j // 2, j % 2

    own = flat_rows(hidden_rows)
    pair = rows_of(own, swap_core(hidden_rows))
    down_other = swap_core(adapter_down_weight)

    k2 = jnp.arange(4, dtype=jnp.int32)[:, None]
    k1 = jnp.arange(4, dtype=jnp.int32)[None, :]
    blocks_of = lambda core: (
        me ^ (16 * core) ^ jnp.where(core == 0, 4 * k1 + k2, 4 * k2 + k1)
    ).reshape(16)
    groups = jnp.concatenate([blocks_of(c), blocks_of(1 - c)])

    start = cross_z(pair)
    low, high = line_halves(start, *[along_x(start, k) for k in (1, 2, 3)])
    low3, high1 = along_y(low, 3), along_y(high, 1)
    q = queries.reshape(rows, -1, HEAD_SIZE)
    top, total, gathered = cached_attention(
        *ready_queries(kv_lengths, q, k_cache.shape[1], start), k_cache, value_cache
    )
    high3, low1 = along_y(high, 3), along_y(low, 1)
    low2, high2 = along_y(low3, 1), along_y(high1, 3)
    blocks = ((low, high), (low1, high1), (low2, high2), (low3, high3))

    codes = make_codes(groups, (me * owned).reshape(1), adapter_ids.reshape(-1, rows), start)
    partial = []
    for k in range(4):
        after = (gathered,) if k == 2 else ()
        partial.append(
            down_block(k, blocks[k], adapter_down_weight, down_other, codes, after)
        )
    partial = jnp.stack(partial)

    chunks = make_chunks(own, low)
    mine = lax.dynamic_index_in_dim(partial, t, 0, keepdims=False).astype(F32)
    came = []
    for m in (1, 2, 3):
        sent = lax.dynamic_index_in_dim(partial, t ^ m, 0, keepdims=False)
        came.append(along_z(jnp.stack([sent, chunks[0][0]]), m))
        mine = mine + came[-1][0].astype(F32)
    both = jnp.stack([mine.astype(BF16), chunks[1][0]])
    slots = [along_z(both, m) for m in (1, 2, 3)]
    wide = widen(adapter_up_weight, both)
    others = swap_core(pack(chunks[0], both, *slots, *came))
    delta = up_blocks(jnp.stack([t, c]), (both, *slots), others, codes, wide)
    full = whole_rows(j.reshape(1), chunks, came, slots, others)

    back = delta[0]
    for k in (1, 3, 2):
        back = back + second_axis(delta[k], k)
    home = back[0]
    for k in (1, 3, 2):
        home = home + first_axis(back[k], k)
    half = full.shape[1] // 2
    base = jnp.dot(full[:, :half], key_value_weight[:half], preferred_element_type=F32)
    kept, sent = small(
        "split",
        split_kernel,
        (jax.ShapeDtypeStruct(home.shape[1:], BF16),) * 2,
        [smem(), vmem(), vmem()],
        (c.reshape(1), home, base),
    )
    came = swap_z(sent)
    base = base + jnp.dot(full[:, half:], key_value_weight[half:], preferred_element_type=F32)

    half = HEAD_SIZE // 2
    frequency = jnp.exp(jnp.arange(half, dtype=F32) * (-2.0 * math.log(500000.0) / HEAD_SIZE))
    positions = (kv_lengths[:, None] + jnp.arange(steps, dtype=jnp.int32)[None, :]).reshape(group)
    angles = positions.astype(F32)[:, None] * frequency
    cosine, sine = jnp.cos(angles), jnp.sin(angles)
    cosine = jnp.concatenate([cosine, cosine], 1)
    sine = jnp.concatenate([-sine, sine], 1)
    return final_merge(base, kept, came, cosine, sine, q, top, total, gathered)


def solution(mesh):
    return jax.shard_map(
        per_device,
        mesh=mesh,
        in_specs=(
            P("dp", None, "tensor"),
            P(None, "tensor"),
            P("dp", "tensor", None),
            P("dp", None, "tensor"),
            P(),
            P("dp"),
            P("dp", None, "tensor"),
            P("dp", None, "tensor"),
            P("dp", None, "tensor"),
        ),
        out_specs=(P("dp", None, "tensor"), P("dp", None, "tensor")),
        check_vma=False,
    )
```
